32 devices in a mesh: row: 8 (over z, y), col: 4 (over x, core).
Axes of the slice: x: 2, y: 2, z: 4, core: 2. Of those that a mesh axis runs over, the one named last changes fastest.
Arguments:
- anc_inverse: bfloat16 [1, 8, 256, 2, 4, 256], P(None, 'row', None, None, 'col'), may hold values from -6 to 6
- factor_one: bfloat16 [1, 8, 256, 2, 4, 256], P(None, 'row', None, None, 'col'), may hold values from -0.125 to 0.125
- factor_two: bfloat16 [1, 8, 256, 1, 4, 256], P(None, 'row', None, None, 'col'), may hold values from -0.125 to 0.125
- parent_block: bfloat16 [1, 4, 256, 256], P(None, 'col'), may hold values from -0.375 to 0.375
- diag_one: float32 [2, 4, 256, 256], P(None, 'col'), may hold values from -6 to 6
- diag_two: float32 [1, 4, 256, 256], P(None, 'col'), may hold values from -6 to 6
- pattern_one: int32 [1, 8, 2, 4], P(None, 'row', None, 'col'), may hold values from 0 to 1
- pattern_two: int32 [1, 8, 1, 4], P(None, 'row', None, 'col'), may hold values from 0 to 1, as said below
- parent: int32 [1, 4], P(None, 'col'), may hold values from 0 to 7, as said below
Outputs:
- inv_one: bfloat16 [1, 8, 256, 2, 4, 256], P(None, 'row', None, None, 'col')
- diag_inv_one: float32 [2, 4, 256, 256], P(None, 'col')
- inv_two: bfloat16 [1, 8, 256, 1, 4, 256], P(None, 'row', None, None, 'col')
- parent_inv: bfloat16 [1, 4, 256, 256], P(None, 'col')
- diag_inv_two: float32 [1, 4, 256, 256], P(None, 'col')
The draws below stay inside these ranges and needn't reach their ends.
Inputs may be any that keep to these rules, and one draw needn't show every extreme that they name: pattern_two[J, K] is zero wherever pattern_one[J, P(K)] is zero. parent[k, c] is a level-one supernode whose index leaves remainder c when divided by 4.
All inputs are finite; a program needn't handle non-finite values.
Results may differ from the reference program's by a relative error of at most 0.007.
Values may be sent and summed in bfloat16 or wider, within the bound.
No kernel may reach another device: no remote copies, remote signals or barrier semaphores. Data moves between devices by JAX's collectives and lax.ppermute only.
A program may use at most 64 MiB of HBM per device.

```python
import jax
import jax.numpy as jnp
from jax import lax

B = 256
AR = 1
PC = 2
CC = 1
NA = 8
NP = 8
NC = 4
N_ROW = 8
N_COL = 4


def tree_draws(key):
    first_mask = jax.random.randint(jax.random.fold_in(key, 101), (AR, N_ROW, PC, N_COL), 0, 2).astype(jnp.int32)
    local_parent = jax.random.randint(jax.random.fold_in(key, 102), (CC, N_COL), 0, PC).astype(jnp.int32)
    local_parent = local_parent.at[0, 0].set(0).at[0, N_COL - 1].set(PC - 1)
    column_ids = jnp.arange(N_COL, dtype=jnp.int32)[None, :]
    parent_ids = local_parent * N_COL + column_ids
    keep_mask = (jax.random.randint(jax.random.fold_in(key, 103), (AR, N_ROW, CC, N_COL), 0, 4) > 0).astype(jnp.int32)
    spread = jnp.broadcast_to(local_parent[None, None], (AR, N_ROW, CC, N_COL))
    above_mask = jnp.take_along_axis(first_mask, spread, axis=2)
    return (first_mask, above_mask * keep_mask, parent_ids)


def draw_pattern_one(key, part):
    return tree_draws(key)[0]


def draw_pattern_two(key, part):
    return tree_draws(key)[1]


def draw_parent(key, part):
    return tree_draws(key)[2]


def shard_levels(stream_key, dims, split, smallest, high):
    factor_of = 1.0
    for position, blocks in split:
        draws = jax.random.uniform(jax.random.fold_in(jax.random.fold_in(stream_key, 6), position), (blocks,), jnp.float32, smallest / len(split), high / len(split))
        factor_of = factor_of * jnp.repeat(jnp.exp(draws), dims[position] // blocks).reshape((-1,) + (1,) * (len(dims) - 1 - position))
    return factor_of


def centred(stream_key, extent, scale, reach, split=(), kind=jnp.bfloat16):
    entries = scale * jax.random.normal(stream_key, extent, jnp.float32)
    if split:
        entries = entries * shard_levels(stream_key, extent, split, -0.22, 0.18)
    return jnp.clip(entries, -reach, reach).astype(kind)


def setup_inputs(seed: int = 0) -> dict:
    splits = jax.random.split(jax.random.key(seed), 10)
    return {
        "anc_inverse": centred(splits[0], (AR, N_ROW, B, NA // N_COL, N_COL, B), 1.0, 6.0, ((1, 8), (4, 4))),
        "factor_one": centred(splits[1], (AR, N_ROW, B, PC, N_COL, B), (NA * B) ** -0.5, 0.125, ((1, 8), (4, 4))),
        "factor_two": centred(splits[2], (AR, N_ROW, B, CC, N_COL, B), (NA * B) ** -0.5, 0.125, ((1, 8), (4, 4))),
        "parent_block": centred(splits[3], (CC, N_COL, B, B), B ** -0.5, 0.375, ((1, 4),)),
        "diag_one": centred(splits[4], (PC, N_COL, B, B), 1.0, 6.0, ((1, 4),), jnp.float32),
        "diag_two": centred(splits[5], (CC, N_COL, B, B), 1.0, 6.0, ((1, 4),), jnp.float32),
        "pattern_one": draw_pattern_one(jax.random.fold_in(splits[9], 71), 0),
        "pattern_two": draw_pattern_two(jax.random.fold_in(splits[9], 71), 0),
        "parent": draw_parent(jax.random.fold_in(splits[9], 71), 0),
    }


def rounded(value):
    return lax.optimization_barrier(value.astype(jnp.bfloat16)).astype(jnp.float32)


def reference(anc_inverse, factor_one, factor_two, parent_block, diag_one, diag_two, pattern_one, pattern_two, parent):
    ancestors = anc_inverse.reshape(NA * B, NA * B)
    first_mask = pattern_one.reshape(NA, 1, NP, 1)
    first_factor = factor_one.reshape(NA, B, NP, B) * first_mask.astype(jnp.bfloat16)
    first_total = jnp.dot(ancestors, first_factor.reshape(NA * B, NP * B), preferred_element_type=jnp.float32)
    first_inv = (-first_total.reshape(NA, B, NP, B) * first_mask.astype(jnp.float32)).astype(jnp.bfloat16)
    first_wide = first_factor.astype(jnp.float32)
    inv_wide = first_inv.astype(jnp.float32)
    first_diag = diag_one.reshape(NP, B, B) - jnp.einsum("ixky,ixkz->kyz", first_wide, inv_wide)
    parent_ids = parent.reshape(NC).astype(jnp.int32)
    second_mask = pattern_two.reshape(NA, 1, NC, 1)
    second_factor = factor_two.reshape(NA, B, NC, B) * second_mask.astype(jnp.bfloat16)
    second_wide = second_factor.astype(jnp.float32)
    parent_cols = jnp.take(inv_wide, parent_ids, axis=2)
    cross = jnp.einsum("ixky,ixkz->kyz", parent_cols, second_wide)
    coupling = parent_block.reshape(NC, B, B).astype(jnp.float32)
    parent_diag = rounded(jnp.take(first_diag, parent_ids, axis=0))
    parent_inv = (-(jnp.einsum("kyx,kxz->kyz", parent_diag, coupling) + cross)).astype(jnp.bfloat16)
    second_total = jnp.dot(ancestors, second_factor.reshape(NA * B, NC * B), preferred_element_type=jnp.float32)
    side = jnp.einsum("ixky,kyz->ixkz", parent_cols, coupling)
    second_inv = (-(second_total.reshape(NA, B, NC, B) + side) * second_mask.astype(jnp.float32)).astype(jnp.bfloat16)
    child_terms = jnp.einsum("ixky,ixkz->kyz", second_wide, second_inv.astype(jnp.float32))
    parent_terms = jnp.einsum("kxy,kxz->kyz", coupling, parent_inv.astype(jnp.float32))
    second_diag = diag_two.reshape(NC, B, B) - (child_terms + parent_terms)
    return (first_inv.reshape(AR, N_ROW, B, PC, N_COL, B), first_diag.reshape(PC, N_COL, B, B), second_inv.reshape(AR, N_ROW, B, CC, N_COL, B), parent_inv.reshape(CC, N_COL, B, B), second_diag.reshape(CC, N_COL, B, B))
```

```python
import functools

import jax
import jax.numpy as jnp
from jax import lax
from jax.experimental import pallas as pl
from jax.experimental.pallas import tpu as pltpu
from jax.sharding import PartitionSpec as P

AXES = ("row", "col")


def send(value, sizes, source):
    high, wide = sizes
    pairs = []
    for z in range(high):
        for y in range(2):
            for x in range(wide):
                for k in range(2):
                    sz, sy, sx, sk = source(z, y, x, k)
                    pairs.append(
                        ((2 * sz + sy) * 2 * wide + 2 * sx + sk, (2 * z + y) * 2 * wide + 2 * x + k)
                    )
    return lax.ppermute(value, AXES, pairs)


def place():
    row, col = lax.axis_index("row"), lax.axis_index("col")
    return row // 2, row % 2, col // 2, col % 2


def tdot(left, right):
    return lax.dot_general(
        left, right, (((0,), (0,)), ((), ())), preferred_element_type=jnp.float32
    )


def product_kernel(high, wide, *refs):
    a_refs = refs[: 2 * wide]
    x_refs = refs[2 * wide : 2 * wide + high]
    other_ref, couple_ref = refs[2 * wide + high : 2 * wide + high + 2]
    keep_y, send_y, keep_g, send_g, a_all, x_all, x_row, y_all, g_all = refs[2 * wide + high + 2 :]
    block = other_ref.shape[0]
    z, y, x, k = place()
    turn = z ^ x
    swap = y ^ k
    for step in range(high):
        x_all[pl.ds(pl.multiple_of((turn ^ step) * block, block), block), :] = x_refs[step][...]
    for dy in range(2):
        for dx in range(wide):
            for kk in range(2):
                t = kk * wide + dx
                a_all[dy * block : (dy + 1) * block, t * block : (t + 1) * block] = a_refs[
                    dy * wide + dx
                ][kk]
    x_row[pl.ds(pl.multiple_of(swap * block, block), block), :] = x_refs[0][...]
    x_row[pl.ds(pl.multiple_of((1 - swap) * block, block), block), :] = other_ref[...]
    total = jnp.dot(a_all[...], x_all[...], preferred_element_type=jnp.float32)
    near = total[:, :block].astype(jnp.bfloat16)
    far = total[:, block : 2 * block]
    last = total[:, 2 * block :] - jnp.dot(
        near, couple_ref[...], preferred_element_type=jnp.float32
    )
    y_all[:, : 2 * block] = total[:, : 2 * block]
    y_all[:, 2 * block :] = last
    g_all[:block] = tdot(x_row[:, :block], near)
    g_all[block : 2 * block] = tdot(x_row[:, block : 2 * block], far.astype(jnp.bfloat16))
    g_all[2 * block : 3 * block] = tdot(near, x_row[:, 2 * block :])
    g_all[3 * block :] = tdot(x_row[:, 2 * block :], last.astype(jnp.bfloat16))
    keep_y[...] = y_all[pl.ds(pl.multiple_of(swap * block, block), block), :]
    send_y[...] = y_all[pl.ds(pl.multiple_of((1 - swap) * block, block), block), :]
    keep_g[...] = g_all[pl.ds(pl.multiple_of(k * 2 * block, block), 2 * block), :]
    send_g[...] = g_all[pl.ds(pl.multiple_of((1 - k) * 2 * block, block), 2 * block), :].astype(
        jnp.bfloat16
    )


def finish_kernel(first_ref, second_ref, one_ref, two_ref, couple_ref, which_ref, out_one, out_parent, out_two, terms):
    block = couple_ref.shape[0]
    z, y, x, k = place()
    terms[y] = first_ref[...].astype(jnp.float32)
    terms[1 - y] = second_ref[...].astype(jnp.float32)
    near = which_ref[0]
    out_one[near] = one_ref[near] + terms[0, :block]
    out_one[1 - near] = one_ref[1 - near] + terms[0, block:]
    couple = couple_ref[...]
    diag = out_one[near].astype(jnp.bfloat16)
    parent = -(jnp.dot(diag, couple, preferred_element_type=jnp.float32) - terms[1, :block])
    parent = parent.astype(jnp.bfloat16)
    out_parent[...] = parent
    out_two[...] = two_ref[...] + terms[1, block:] - tdot(couple, parent)


def body(
    anc_inverse,
    factor_one,
    factor_two,
    parent_block,
    diag_one,
    diag_two,
    pattern_one,
    pattern_two,
    parent,
):
    block = anc_inverse.shape[2]
    high = lax.axis_size("row") // 2
    wide = lax.axis_size("col") // 2
    sizes = (high, wide)
    z, y, x, k = place()
    near = parent.reshape(1) // lax.axis_size("col")
    keep_one = pattern_one.reshape(2)
    keep_two = pattern_two.reshape(1)
    flip = near[0] == 1
    one = factor_one.reshape(block, 2, block)
    two = factor_two.reshape(block, block)
    masked = one * keep_one.astype(jnp.bfloat16)[None, :, None]
    zero, unit = masked[:, 0], masked[:, 1]
    cols = jnp.concatenate(
        [
            jnp.where(flip, unit, zero),
            jnp.where(flip, zero, unit),
            two * keep_two.astype(jnp.bfloat16)[0],
        ],
        axis=1,
    )
    coupling = parent_block.reshape(block, block)
    anc = anc_inverse.reshape(block, 2, block).transpose(1, 0, 2)

    pieces = [
        send(cols, sizes, lambda z, y, x, k, d=d: (z ^ d, k, x, y)) for d in range(high)
    ]
    couple = send(coupling, sizes, lambda z, y, x, k: (z, k, x, y))
    other = send(pieces[0], sizes, lambda z, y, x, k: (z, y, x, 1 - k))
    ancs = [
        anc
        if dy == 0 and dx == 0
        else send(anc, sizes, lambda z, y, x, k, dy=dy, dx=dx: (z, y ^ dy, x ^ dx, k))
        for dy in range(2)
        for dx in range(wide)
    ]
    width = 3 * block
    keep_y, send_y, keep_g, send_g = pl.pallas_call(
        functools.partial(product_kernel, high, wide),
        out_shape=(
            jax.ShapeDtypeStruct((block, width), jnp.float32),
            jax.ShapeDtypeStruct((block, width), jnp.float32),
            jax.ShapeDtypeStruct((2 * block, block), jnp.float32),
            jax.ShapeDtypeStruct((2 * block, block), jnp.bfloat16),
        ),
        scratch_shapes=[
            pltpu.VMEM((2 * block, high * block), jnp.bfloat16),
            pltpu.VMEM((high * block, width), jnp.bfloat16),
            pltpu.VMEM((2 * block, width), jnp.bfloat16),
            pltpu.VMEM((2 * block, width), jnp.float32),
            pltpu.VMEM((4 * block, block), jnp.float32),
        ],
        compiler_params=pltpu.CompilerParams(vmem_limit_bytes=48 * 1024 * 1024),
        name="products",
    )(*ancs, *pieces, other, couple)

    def core_swap(value):
        return send(value, sizes, lambda z, y, x, k: (z, y, x, 1 - k))

    mine = keep_g + core_swap(send_g).astype(jnp.float32)
    rows = 2 * block // high

    def part(value, at):
        return lax.dynamic_slice_in_dim(value, at * rows, rows, axis=0)

    coarse = mine.astype(jnp.bfloat16)
    share = part(mine, z)
    for d in range(1, high):
        got = send(part(coarse, z ^ d), sizes, lambda z, y, x, k, d=d: (z ^ d, y, x, k))
        share = share + got.astype(jnp.float32)
    share = share.astype(jnp.bfloat16)
    half = jnp.zeros((2 * block, block), jnp.bfloat16)
    half = lax.dynamic_update_slice_in_dim(half, share, z * rows, axis=0)
    for d in range(1, high):
        got = send(share, sizes, lambda z, y, x, k, d=d: (z ^ d, y, x, k))
        half = lax.dynamic_update_slice_in_dim(half, got, (z ^ d) * rows, axis=0)
    first = send(half, sizes, lambda z, y, x, k: (z, k, x, y))
    second = send(half, sizes, lambda z, y, x, k: (z, k, x, 1 - y))

    row_y = (keep_y + core_swap(send_y)).astype(jnp.bfloat16)
    row_y = send(row_y, sizes, lambda z, y, x, k: (z, k, x, y))
    near_y, far_y, last_y = row_y[:, :block], row_y[:, block : 2 * block], row_y[:, 2 * block :]
    inv_zero = jnp.where(flip, far_y, near_y)
    inv_unit = jnp.where(flip, near_y, far_y)
    inv_one = jnp.stack([inv_zero, inv_unit], axis=1) * -keep_one.astype(jnp.bfloat16)[None, :, None]
    inv_two = last_y * -keep_two.astype(jnp.bfloat16)[0]

    out_one, out_parent, out_two = pl.pallas_call(
        finish_kernel,
        out_shape=(
            jax.ShapeDtypeStruct((2, block, block), jnp.float32),
            jax.ShapeDtypeStruct((block, block), jnp.bfloat16),
            jax.ShapeDtypeStruct((block, block), jnp.float32),
        ),
        in_specs=[pl.BlockSpec(memory_space=pltpu.VMEM)] * 5
        + [pl.BlockSpec(memory_space=pltpu.SMEM)],
        scratch_shapes=[pltpu.VMEM((2, 2 * block, block), jnp.float32)],
        name="finish",
    )(
        first,
        second,
        diag_one.reshape(2, block, block),
        diag_two.reshape(block, block),
        coupling,
        near.astype(jnp.int32),
    )
    return (
        inv_one.reshape(factor_one.shape),
        out_one.reshape(diag_one.shape),
        inv_two.reshape(factor_two.shape),
        out_parent.reshape(parent_block.shape),
        out_two.reshape(diag_two.shape),
    )


def solution(mesh):
    placed = (
        P(None, "row", None, None, "col", None),
        P(None, "row", None, None, "col", None),
        P(None, "row", None, None, "col", None),
        P(None, "col", None, None),
        P(None, "col", None, None),
        P(None, "col", None, None),
        P(None, "row", None, "col"),
        P(None, "row", None, "col"),
        P(None, "col"),
    )
    return jax.shard_map(
        body,
        mesh=mesh,
        in_specs=placed,
        out_specs=(
            P(None, "row", None, None, "col", None),
            P(None, "col", None, None),
            P(None, "row", None, None, "col", None),
            P(None, "col", None, None),
            P(None, "col", None, None),
        ),
        check_vma=False,
    )
```

```python
import functools

import jax
import jax.numpy as jnp
from jax import lax
from jax.experimental import pallas as pl
from jax.experimental.pallas import tpu as pltpu
from jax.sharding import PartitionSpec as P

AXES = ("row", "col")


def send(value, sizes, source):
    high, wide = sizes
    pairs = []
    for z in range(high):
        for y in range(2):
            for x in range(wide):
                for k in range(2):
                    sz, sy, sx, sk = source(z, y, x, k)
                    pairs.append(
                        ((2 * sz + sy) * 2 * wide + 2 * sx + sk, (2 * z + y) * 2 * wide + 2 * x + k)
                    )
    return lax.ppermute(value, AXES, pairs)


def place():
    row, col = lax.axis_index("row"), lax.axis_index("col")
    return row // 2, row % 2, col // 2, col % 2


def tdot(left, right):
    return lax.dot_general(
        left, right, (((0,), (0,)), ((), ())), preferred_element_type=jnp.float32
    )


def product_kernel(high, wide, *refs):
    a_refs = refs[: 2 * wide]
    x_refs = refs[2 * wide : 2 * wide + high]
    other_ref, couple_ref = refs[2 * wide + high : 2 * wide + high + 2]
    keep_y, send_y, keep_g, send_g, a_all, x_all, x_row, y_all, g_all = refs[2 * wide + high + 2 :]
    block = other_ref.shape[0]
    z, y, x, k = place()
    low = z % 2
    turn = z ^ x
    swap = y ^ k
    for step in range(high):
        x_all[pl.ds(pl.multiple_of((turn ^ step) * block, block), block), :] = x_refs[step][...]
    for dy in range(2):
        for dx in range(wide):
            for kk in range(2):
                t = kk * wide + dx
                a_all[dy * block : (dy + 1) * block, t * block : (t + 1) * block] = a_refs[
                    dy * wide + dx
                ][kk]
    x_row[pl.ds(pl.multiple_of(swap * block, block), block), :] = x_refs[0][...]
    x_row[pl.ds(pl.multiple_of((1 - swap) * block, block), block), :] = other_ref[...]
    total = jnp.dot(a_all[...], x_all[...], preferred_element_type=jnp.float32)
    near = total[:, :block].astype(jnp.bfloat16)
    far = total[:, block : 2 * block]
    last = total[:, 2 * block :] - jnp.dot(
        near, couple_ref[...], preferred_element_type=jnp.float32
    )
    y_all[:, : 2 * block] = total[:, : 2 * block]
    y_all[:, 2 * block :] = last
    g_all[0] = tdot(x_row[:, :block], near)
    g_all[1] = tdot(x_row[:, block : 2 * block], far.astype(jnp.bfloat16))
    g_all[2] = tdot(near, x_row[:, 2 * block :])
    g_all[3] = tdot(x_row[:, 2 * block :], last.astype(jnp.bfloat16))
    keep_y[...] = y_all[pl.ds(pl.multiple_of(swap * block, block), block), :]
    send_y[...] = y_all[pl.ds(pl.multiple_of((1 - swap) * block, block), block), :]
    keep_g[:block] = g_all[2 * k + low]
    keep_g[block:] = g_all[2 * k + 1 - low]
    send_g[:block] = g_all[2 * (1 - k) + low].astype(jnp.bfloat16)
    send_g[block:] = g_all[2 * (1 - k) + 1 - low].astype(jnp.bfloat16)


def finish_kernel(*refs):
    got_refs = refs[:4]
    one_ref, two_ref, couple_ref, which_ref, out_one, out_parent, out_two, terms = refs[4:]
    z, y, x, k = place()
    low = z % 2
    for i, ref in enumerate(got_refs):
        terms[2 * (y ^ (i % 2)) + (low ^ (i // 2))] = ref[...].astype(jnp.float32)
    near = which_ref[0]
    one = one_ref[near] + terms[0]
    out_one[near] = one
    out_one[1 - near] = one_ref[1 - near] + terms[1]
    couple = couple_ref[...]
    parent = -(
        jnp.dot(one.astype(jnp.bfloat16), couple, preferred_element_type=jnp.float32) - terms[2]
    )
    parent = parent.astype(jnp.bfloat16)
    out_parent[...] = parent
    out_two[...] = two_ref[...] + terms[3] - tdot(couple, parent)


def body(
    anc_inverse,
    factor_one,
    factor_two,
    parent_block,
    diag_one,
    diag_two,
    pattern_one,
    pattern_two,
    parent,
):
    block = anc_inverse.shape[2]
    high = lax.axis_size("row") // 2
    wide = lax.axis_size("col") // 2
    sizes = (high, wide)
    z, y, x, k = place()
    near = parent.reshape(1) // lax.axis_size("col")
    keep_one = pattern_one.reshape(2)
    keep_two = pattern_two.reshape(1)
    flip = near[0] == 1
    one = factor_one.reshape(block, 2, block)
    two = factor_two.reshape(block, block)
    masked = one * keep_one.astype(jnp.bfloat16)[None, :, None]
    zero, unit = masked[:, 0], masked[:, 1]
    cols = jnp.concatenate(
        [
            jnp.where(flip, unit, zero),
            jnp.where(flip, zero, unit),
            two * keep_two.astype(jnp.bfloat16)[0],
        ],
        axis=1,
    )
    coupling = parent_block.reshape(block, block)
    anc = anc_inverse.reshape(block, 2, block).transpose(1, 0, 2)

    pieces = [
        send(cols, sizes, lambda z, y, x, k, d=d: (z ^ d, k, x, y)) for d in range(high)
    ]
    couple = send(coupling, sizes, lambda z, y, x, k: (z, k, x, y))
    other = send(pieces[0], sizes, lambda z, y, x, k: (z, y, x, 1 - k))
    ancs = [
        anc
        if dy == 0 and dx == 0
        else send(anc, sizes, lambda z, y, x, k, dy=dy, dx=dx: (z, y ^ dy, x ^ dx, k))
        for dy in range(2)
        for dx in range(wide)
    ]
    width = 3 * block
    keep_y, send_y, keep_g, send_g = pl.pallas_call(
        functools.partial(product_kernel, high, wide),
        out_shape=(
            jax.ShapeDtypeStruct((block, width), jnp.float32),
            jax.ShapeDtypeStruct((block, width), jnp.float32),
            jax.ShapeDtypeStruct((2 * block, block), jnp.float32),
            jax.ShapeDtypeStruct((2 * block, block), jnp.bfloat16),
        ),
        scratch_shapes=[
            pltpu.VMEM((2 * block, high * block), jnp.bfloat16),
            pltpu.VMEM((high * block, width), jnp.bfloat16),
            pltpu.VMEM((2 * block, width), jnp.bfloat16),
            pltpu.VMEM((2 * block, width), jnp.float32),
            pltpu.VMEM((4, block, block), jnp.float32),
        ],
        compiler_params=pltpu.CompilerParams(vmem_limit_bytes=48 * 1024 * 1024),
        name="products",
    )(*ancs, *pieces, other, couple)

    def core_swap(value):
        return send(value, sizes, lambda z, y, x, k: (z, y, x, 1 - k))

    def along(value, d):
        return send(value, sizes, lambda z, y, x, k: (z ^ d, y, x, k))

    chip = keep_g + core_swap(send_g).astype(jnp.float32)
    total = chip[:block] + along(chip[block:].astype(jnp.bfloat16), 1).astype(jnp.float32)
    total = total.astype(jnp.bfloat16)
    d = 2
    while d < high:
        total = (total.astype(jnp.float32) + along(total, d).astype(jnp.float32)).astype(jnp.bfloat16)
        d *= 2
    terms = [
        send(total, sizes, lambda z, y, x, k, d=d, e=e: (z ^ d, k, x, y ^ e))
        for d in range(2)
        for e in range(2)
    ]

    row_y = (keep_y + core_swap(send_y)).astype(jnp.bfloat16)
    row_y = send(row_y, sizes, lambda z, y, x, k: (z, k, x, y))
    near_y, far_y, last_y = row_y[:, :block], row_y[:, block : 2 * block], row_y[:, 2 * block :]
    inv_zero = jnp.where(flip, far_y, near_y)
    inv_unit = jnp.where(flip, near_y, far_y)
    inv_one = jnp.stack([inv_zero, inv_unit], axis=1) * -keep_one.astype(jnp.bfloat16)[None, :, None]
    inv_two = last_y * -keep_two.astype(jnp.bfloat16)[0]

    out_one, out_parent, out_two = pl.pallas_call(
        finish_kernel,
        out_shape=(
            jax.ShapeDtypeStruct((2, block, block), jnp.float32),
            jax.ShapeDtypeStruct((block, block), jnp.bfloat16),
            jax.ShapeDtypeStruct((block, block), jnp.float32),
        ),
        in_specs=[pl.BlockSpec(memory_space=pltpu.VMEM)] * 7
        + [pl.BlockSpec(memory_space=pltpu.SMEM)],
        scratch_shapes=[pltpu.VMEM((4, block, block), jnp.float32)],
        name="finish",
    )(
        *terms,
        diag_one.reshape(2, block, block),
        diag_two.reshape(block, block),
        coupling,
        near.astype(jnp.int32),
    )
    return (
        inv_one.reshape(factor_one.shape),
        out_one.reshape(diag_one.shape),
        inv_two.reshape(factor_two.shape),
        out_parent.reshape(parent_block.shape),
        out_two.reshape(diag_two.shape),
    )


def solution(mesh):
    placed = (
        P(None, "row", None, None, "col", None),
        P(None, "row", None, None, "col", None),
        P(None, "row", None, None, "col", None),
        P(None, "col", None, None),
        P(None, "col", None, None),
        P(None, "col", None, None),
        P(None, "row", None, "col"),
        P(None, "row", None, "col"),
        P(None, "col"),
    )
    return jax.shard_map(
        body,
        mesh=mesh,
        in_specs=placed,
        out_specs=(
            P(None, "row", None, None, "col", None),
            P(None, "col", None, None),
            P(None, "row", None, None, "col", None),
            P(None, "col", None, None),
            P(None, "col", None, None),
        ),
        check_vma=False,
    )
```

```python
import functools

import jax
import jax.numpy as jnp
from jax import lax
from jax.experimental import pallas as pl
from jax.experimental.pallas import tpu as pltpu
from jax.sharding import PartitionSpec as P

AXES = ("row", "col")


def send(value, sizes, source):
    high, wide = sizes
    pairs = []
    for z in range(high):
        for y in range(2):
            for x in range(wide):
                for k in range(2):
                    sz, sy, sx, sk = source(z, y, x, k)
                    pairs.append(
                        ((2 * sz + sy) * 2 * wide + 2 * sx + sk, (2 * z + y) * 2 * wide + 2 * x + k)
                    )
    return lax.ppermute(value, AXES, pairs)


def place():
    row, col = lax.axis_index("row"), lax.axis_index("col")
    return row // 2, row % 2, col // 2, col % 2


def tdot(left, right):
    return lax.dot_general(
        left, right, (((0,), (0,)), ((), ())), preferred_element_type=jnp.float32
    )


def product_kernel(high, wide, *refs):
    near_refs, far_ref = refs[:wide], refs[wide]
    refs = refs[wide + 1 :]
    x_refs, other_ref = refs[:high], refs[high]
    keep_y, send_y, keep_g, send_g, a_all, x_all, x_row, y_all, g_all = refs[high + 1 :]
    block = other_ref.shape[0]
    z, y, x, k = place()
    low = z % 2
    turn = z ^ x
    swap = y ^ k
    width = 3 * block
    couple = x_refs[0][:, width:]
    for step in range(high):
        x_all[pl.ds(pl.multiple_of((turn ^ step) * block, block), block), :] = x_refs[step][:, :width]
    for dy in range(2):
        for dx in range(wide):
            for kk in range(2):
                t = kk * wide + dx
                a_all[dy * block : (dy + 1) * block, t * block : (t + 1) * block] = (
                    far_ref[dx, kk] if dy else near_refs[dx][kk]
                )
    x_row[pl.ds(pl.multiple_of(swap * block, block), block), :] = x_refs[0][:, :width]
    x_row[pl.ds(pl.multiple_of((1 - swap) * block, block), block), :] = other_ref[:, :width]
    total = jnp.dot(a_all[...], x_all[...], preferred_element_type=jnp.float32)
    near = total[:, :block].astype(jnp.bfloat16)
    far = total[:, block : 2 * block]
    last = total[:, 2 * block :] - jnp.dot(
        near, couple, preferred_element_type=jnp.float32
    )
    y_all[:, : 2 * block] = total[:, : 2 * block]
    y_all[:, 2 * block :] = last
    g_all[0] = tdot(x_row[:, :block], near)
    g_all[1] = tdot(x_row[:, block : 2 * block], far.astype(jnp.bfloat16))
    g_all[2] = tdot(near, x_row[:, 2 * block :])
    g_all[3] = tdot(x_row[:, 2 * block :], last.astype(jnp.bfloat16))
    keep_y[...] = y_all[pl.ds(pl.multiple_of(swap * block, block), block), :]
    send_y[...] = y_all[pl.ds(pl.multiple_of((1 - swap) * block, block), block), :]
    keep_g[:block] = g_all[2 * k + low]
    keep_g[block:] = g_all[2 * k + 1 - low]
    send_g[:block] = g_all[2 * (1 - k) + low].astype(jnp.bfloat16)
    send_g[block:] = g_all[2 * (1 - k) + 1 - low].astype(jnp.bfloat16)


def finish_kernel(*refs):
    got_refs = refs[:4]
    one_ref, two_ref, couple_ref, which_ref, out_one, out_parent, out_two, terms = refs[4:]
    z, y, x, k = place()
    low = z % 2
    for i, ref in enumerate(got_refs):
        terms[2 * (y ^ (i % 2)) + (low ^ (i // 2))] = ref[...].astype(jnp.float32)
    near = which_ref[0]
    one = one_ref[near] + terms[0]
    out_one[near] = one
    out_one[1 - near] = one_ref[1 - near] + terms[1]
    couple = couple_ref[...]
    parent = -(
        jnp.dot(one.astype(jnp.bfloat16), couple, preferred_element_type=jnp.float32) - terms[2]
    )
    parent = parent.astype(jnp.bfloat16)
    out_parent[...] = parent
    out_two[...] = two_ref[...] + terms[3] - tdot(couple, parent)


def body(
    anc_inverse,
    factor_one,
    factor_two,
    parent_block,
    diag_one,
    diag_two,
    pattern_one,
    pattern_two,
    parent,
):
    block = anc_inverse.shape[2]
    high = lax.axis_size("row") // 2
    wide = lax.axis_size("col") // 2
    sizes = (high, wide)
    z, y, x, k = place()
    near = parent.reshape(1) // lax.axis_size("col")
    keep_one = pattern_one.reshape(2)
    keep_two = pattern_two.reshape(1)
    flip = near[0] == 1
    one = factor_one.reshape(block, 2, block)
    zero = one[:, 0] * keep_one[0].astype(jnp.bfloat16)
    unit = one[:, 1] * keep_one[1].astype(jnp.bfloat16)
    pair = jnp.concatenate([jnp.where(flip, unit, zero), jnp.where(flip, zero, unit)], axis=1)
    last = factor_two.reshape(block, block) * keep_two[0].astype(jnp.bfloat16)
    cols = jnp.concatenate([pair, last], axis=1)
    coupling = parent_block.reshape(block, block)
    anc = anc_inverse.reshape(block, 2, block).transpose(1, 0, 2)

    def plane(value, dy, dx):
        return send(value, sizes, lambda z, y, x, k: (z, y ^ dy, x ^ dx, k))

    def across(value, d):
        return send(value, sizes, lambda z, y, x, k: (z ^ d, k, x, y))

    def beside(value):
        return send(value, sizes, lambda z, y, x, k: (z ^ 1, y, x, k))

    pieces = {d: across(cols, d) for d in [*range(2, high, 2), 1]}
    own = across(jnp.concatenate([cols, coupling], axis=1), 0)
    now = anc
    near_anc = [anc] + [plane(now, 0, dx) for dx in range(1, wide)]
    stacked = jnp.stack(near_anc)
    far_anc = plane(stacked, 1, 0)
    for d in range(3, high, 2):
        pieces[d] = beside(pieces[d - 1])
    pieces[1], own_now = lax.optimization_barrier((pieces[1], own))
    other = send(own_now, sizes, lambda z, y, x, k: (z, y, x, 1 - k))
    pieces = [own] + [pieces[d] for d in range(1, high)]
    width = 3 * block
    keep_y, send_y, keep_g, send_g = pl.pallas_call(
        functools.partial(product_kernel, high, wide),
        out_shape=(
            jax.ShapeDtypeStruct((block, width), jnp.float32),
            jax.ShapeDtypeStruct((block, width), jnp.float32),
            jax.ShapeDtypeStruct((2 * block, block), jnp.float32),
            jax.ShapeDtypeStruct((2 * block, block), jnp.bfloat16),
        ),
        scratch_shapes=[
            pltpu.VMEM((2 * block, high * block), jnp.bfloat16),
            pltpu.VMEM((high * block, width), jnp.bfloat16),
            pltpu.VMEM((2 * block, width), jnp.bfloat16),
            pltpu.VMEM((2 * block, width), jnp.float32),
            pltpu.VMEM((4, block, block), jnp.float32),
        ],
        compiler_params=pltpu.CompilerParams(vmem_limit_bytes=48 * 1024 * 1024),
        name="products",
    )(*near_anc, far_anc, *pieces, other)

    def core_swap(value):
        return send(value, sizes, lambda z, y, x, k: (z, y, x, 1 - k))

    def along(value, d):
        return send(value, sizes, lambda z, y, x, k: (z ^ d, y, x, k))

    chip = keep_g + core_swap(send_g).astype(jnp.float32)
    total = chip[:block] + along(chip[block:].astype(jnp.bfloat16), 1).astype(jnp.float32)
    total = total.astype(jnp.bfloat16)
    d = 2
    while d < high:
        total = (total.astype(jnp.float32) + along(total, d).astype(jnp.float32)).astype(jnp.bfloat16)
        d *= 2
    terms = [
        send(total, sizes, lambda z, y, x, k, d=d, e=e: (z ^ d, k, x, y ^ e))
        for d in range(2)
        for e in range(2)
    ]

    row_y = (keep_y + core_swap(send_y)).astype(jnp.bfloat16)
    row_y = send(row_y, sizes, lambda z, y, x, k: (z, k, x, y))
    near_y, far_y, last_y = row_y[:, :block], row_y[:, block : 2 * block], row_y[:, 2 * block :]
    inv_zero = jnp.where(flip, far_y, near_y)
    inv_unit = jnp.where(flip, near_y, far_y)
    inv_one = jnp.stack([inv_zero, inv_unit], axis=1) * -keep_one.astype(jnp.bfloat16)[None, :, None]
    inv_two = last_y * -keep_two.astype(jnp.bfloat16)[0]

    out_one, out_parent, out_two = pl.pallas_call(
        finish_kernel,
        out_shape=(
            jax.ShapeDtypeStruct((2, block, block), jnp.float32),
            jax.ShapeDtypeStruct((block, block), jnp.bfloat16),
            jax.ShapeDtypeStruct((block, block), jnp.float32),
        ),
        in_specs=[pl.BlockSpec(memory_space=pltpu.VMEM)] * 7
        + [pl.BlockSpec(memory_space=pltpu.SMEM)],
        scratch_shapes=[pltpu.VMEM((4, block, block), jnp.float32)],
        name="finish",
    )(
        *terms,
        diag_one.reshape(2, block, block),
        diag_two.reshape(block, block),
        coupling,
        near.astype(jnp.int32),
    )
    return (
        inv_one.reshape(factor_one.shape),
        out_one.reshape(diag_one.shape),
        inv_two.reshape(factor_two.shape),
        out_parent.reshape(parent_block.shape),
        out_two.reshape(diag_two.shape),
    )


def solution(mesh):
    placed = (
        P(None, "row", None, None, "col", None),
        P(None, "row", None, None, "col", None),
        P(None, "row", None, None, "col", None),
        P(None, "col", None, None),
        P(None, "col", None, None),
        P(None, "col", None, None),
        P(None, "row", None, "col"),
        P(None, "row", None, "col"),
        P(None, "col"),
    )
    return jax.shard_map(
        body,
        mesh=mesh,
        in_specs=placed,
        out_specs=(
            P(None, "row", None, None, "col", None),
            P(None, "col", None, None),
            P(None, "row", None, None, "col", None),
            P(None, "col", None, None),
            P(None, "col", None, None),
        ),
        check_vma=False,
    )
```

```python
import functools

import jax
import jax.numpy as jnp
from jax import lax
from jax.experimental import pallas as pl
from jax.experimental.pallas import tpu as pltpu
from jax.sharding import PartitionSpec as P

AXES = ("row", "col")


def send(value, sizes, source):
    high, wide = sizes
    pairs = []
    for z in range(high):
        for y in range(2):
            for x in range(wide):
                for k in range(2):
                    sz, sy, sx, sk = source(z, y, x, k)
                    pairs.append(
                        ((2 * sz + sy) * 2 * wide + 2 * sx + sk, (2 * z + y) * 2 * wide + 2 * x + k)
                    )
    return lax.ppermute(value, AXES, pairs)


def place():
    row, col = lax.axis_index("row"), lax.axis_index("col")
    return row // 2, row % 2, col // 2, col % 2


def tdot(left, right):
    return lax.dot_general(
        left, right, (((0,), (0,)), ((), ())), preferred_element_type=jnp.float32
    )


def product_kernel(high, wide, *refs):
    near_refs, far_refs = refs[:2], refs[2 : wide + 1]
    refs = refs[wide + 1 :]
    x_refs, other_ref = refs[:high], refs[high]
    keep_y, send_y, keep_g, send_g, a_all, x_all, x_row, y_all, g_all = refs[high + 1 :]
    block = other_ref.shape[0]
    z, y, x, k = place()
    low = z % 2
    turn = z ^ x
    swap = y ^ k
    width = 3 * block
    couple = x_refs[0][:, width:]
    for step in range(high):
        x_all[pl.ds(pl.multiple_of((turn ^ step) * block, block), block), :] = x_refs[step][:, :width]
    for dy in range(2):
        for dx in range(wide):
            for kk in range(2):
                t = kk * wide + dx
                a_all[dy * block : (dy + 1) * block, t * block : (t + 1) * block] = (
                    far_refs[dx - 1][dy, kk] if dx else near_refs[dy][kk]
                )
    x_row[pl.ds(pl.multiple_of(swap * block, block), block), :] = x_refs[0][:, :width]
    x_row[pl.ds(pl.multiple_of((1 - swap) * block, block), block), :] = other_ref[:, :width]
    total = jnp.dot(a_all[...], x_all[...], preferred_element_type=jnp.float32)
    near = total[:, :block].astype(jnp.bfloat16)
    far = total[:, block : 2 * block]
    last = total[:, 2 * block :] - jnp.dot(
        near, couple, preferred_element_type=jnp.float32
    )
    y_all[:, : 2 * block] = total[:, : 2 * block]
    y_all[:, 2 * block :] = last
    g_all[0] = tdot(x_row[:, :block], near)
    g_all[1] = tdot(x_row[:, block : 2 * block], far.astype(jnp.bfloat16))
    g_all[2] = tdot(near, x_row[:, 2 * block :])
    g_all[3] = tdot(x_row[:, 2 * block :], last.astype(jnp.bfloat16))
    keep_y[...] = y_all[pl.ds(pl.multiple_of(swap * block, block), block), :]
    send_y[...] = y_all[pl.ds(pl.multiple_of((1 - swap) * block, block), block), :]
    keep_g[:block] = g_all[2 * k + low]
    keep_g[block:] = g_all[2 * k + 1 - low]
    send_g[:block] = g_all[2 * (1 - k) + low].astype(jnp.bfloat16)
    send_g[block:] = g_all[2 * (1 - k) + 1 - low].astype(jnp.bfloat16)


def inverse_kernel(y_ref, which_ref, one_ref, two_ref, out_one, out_two):
    block = y_ref.shape[0]
    flip = which_ref[0] == 1
    near, far = y_ref[:, :block], y_ref[:, block : 2 * block]
    zero = jnp.where(flip, far, near)
    unit = jnp.where(flip, near, far)
    out_one[:, 0, :] = jnp.where(one_ref[0] != 0, -zero, jnp.zeros_like(zero))
    out_one[:, 1, :] = jnp.where(one_ref[1] != 0, -unit, jnp.zeros_like(unit))
    last = y_ref[:, 2 * block :]
    out_two[...] = jnp.where(two_ref[0] != 0, -last, jnp.zeros_like(last))


def finish_kernel(*refs):
    got_refs = refs[:4]
    one_ref, two_ref, couple_ref, which_ref, out_one, out_parent, out_two, terms = refs[4:]
    z, y, x, k = place()
    low = z % 2
    for i, ref in enumerate(got_refs):
        terms[2 * (y ^ (i % 2)) + (low ^ (i // 2))] = ref[...].astype(jnp.float32)
    near = which_ref[0]
    one = one_ref[near] + terms[0]
    out_one[near] = one
    out_one[1 - near] = one_ref[1 - near] + terms[1]
    couple = couple_ref[...]
    parent = -(
        jnp.dot(one.astype(jnp.bfloat16), couple, preferred_element_type=jnp.float32) - terms[2]
    )
    parent = parent.astype(jnp.bfloat16)
    out_parent[...] = parent
    out_two[...] = two_ref[...] + terms[3] - tdot(couple, parent)


def body(
    anc_inverse,
    factor_one,
    factor_two,
    parent_block,
    diag_one,
    diag_two,
    pattern_one,
    pattern_two,
    parent,
):
    block = anc_inverse.shape[2]
    high = lax.axis_size("row") // 2
    wide = lax.axis_size("col") // 2
    sizes = (high, wide)
    z, y, x, k = place()
    near = parent.reshape(1) // lax.axis_size("col")
    keep_one = pattern_one.reshape(2)
    keep_two = pattern_two.reshape(1)
    flip = near[0] == 1
    one = factor_one.reshape(block, 2, block)
    one = jnp.where(keep_one[None, :, None] != 0, one, jnp.bfloat16(0))
    zero, unit = one[:, 0], one[:, 1]
    pair = jnp.concatenate([jnp.where(flip, unit, zero), jnp.where(flip, zero, unit)], axis=1)
    last = factor_two.reshape(block, block) * keep_two[0].astype(jnp.bfloat16)
    cols = jnp.concatenate([pair, last], axis=1)
    coupling = parent_block.reshape(block, block)
    anc = anc_inverse.reshape(block, 2, block).transpose(1, 0, 2)

    def plane(value, dy, dx):
        return send(value, sizes, lambda z, y, x, k: (z, y ^ dy, x ^ dx, k))

    def across(value, d):
        return send(value, sizes, lambda z, y, x, k: (z ^ d, k, x, y))

    def beside(value):
        return send(value, sizes, lambda z, y, x, k: (z ^ 1, y, x, k))

    pieces = {d: across(cols, d) for d in [*range(2, high, 2), 1]}
    own = across(jnp.concatenate([cols, coupling], axis=1), 0)
    now = anc
    near_anc = [anc, plane(now, 1, 0)]
    stacked = jnp.stack(near_anc)
    far_anc = [plane(stacked, 0, dx) for dx in range(1, wide)]
    for d in range(3, high, 2):
        pieces[d] = beside(pieces[d - 1])
    cols_now = cols
    other = send(cols_now, sizes, lambda z, y, x, k: (z, 1 - k, x, y))
    pieces = [own] + [pieces[d] for d in range(1, high)]
    width = 3 * block
    keep_y, send_y, keep_g, send_g = pl.pallas_call(
        functools.partial(product_kernel, high, wide),
        out_shape=(
            jax.ShapeDtypeStruct((block, width), jnp.float32),
            jax.ShapeDtypeStruct((block, width), jnp.float32),
            jax.ShapeDtypeStruct((2 * block, block), jnp.float32),
            jax.ShapeDtypeStruct((2 * block, block), jnp.bfloat16),
        ),
        scratch_shapes=[
            pltpu.VMEM((2 * block, high * block), jnp.bfloat16),
            pltpu.VMEM((high * block, width), jnp.bfloat16),
            pltpu.VMEM((2 * block, width), jnp.bfloat16),
            pltpu.VMEM((2 * block, width), jnp.float32),
            pltpu.VMEM((4, block, block), jnp.float32),
        ],
        compiler_params=pltpu.CompilerParams(vmem_limit_bytes=48 * 1024 * 1024),
        name="products",
    )(*near_anc, *far_anc, *pieces, other)

    def core_swap(value):
        return send(value, sizes, lambda z, y, x, k: (z, y, x, 1 - k))

    def along(value, d):
        return send(value, sizes, lambda z, y, x, k: (z ^ d, y, x, k))

    chip = keep_g + core_swap(send_g).astype(jnp.float32)
    total = chip[:block] + along(chip[block:].astype(jnp.bfloat16), 1).astype(jnp.float32)
    total = total.astype(jnp.bfloat16)
    d = 2
    while d < high:
        total = (total.astype(jnp.float32) + along(total, d).astype(jnp.float32)).astype(jnp.bfloat16)
        d *= 2
    terms = [
        send(total, sizes, lambda z, y, x, k, d=d, e=e: (z ^ d, k, x, y ^ e))
        for d in range(2)
        for e in range(2)
    ]

    row_y = (keep_y + core_swap(send_y)).astype(jnp.bfloat16)
    row_y = send(row_y, sizes, lambda z, y, x, k: (z, k, x, y))
    inv_one, inv_two = pl.pallas_call(
        inverse_kernel,
        out_shape=(
            jax.ShapeDtypeStruct((block, 2, block), jnp.bfloat16),
            jax.ShapeDtypeStruct((block, block), jnp.bfloat16),
        ),
        in_specs=[pl.BlockSpec(memory_space=pltpu.VMEM)] + [pl.BlockSpec(memory_space=pltpu.SMEM)] * 3,
        compiler_params=pltpu.CompilerParams(vmem_limit_bytes=8 * 1024 * 1024),
        name="inverse",
    )(row_y, near.astype(jnp.int32), keep_one, keep_two)
    terms[0], inv_one, inv_two = lax.optimization_barrier((terms[0], inv_one, inv_two))

    out_one, out_parent, out_two = pl.pallas_call(
        finish_kernel,
        out_shape=(
            jax.ShapeDtypeStruct((2, block, block), jnp.float32),
            jax.ShapeDtypeStruct((block, block), jnp.bfloat16),
            jax.ShapeDtypeStruct((block, block), jnp.float32),
        ),
        in_specs=[pl.BlockSpec(memory_space=pltpu.VMEM)] * 7
        + [pl.BlockSpec(memory_space=pltpu.SMEM)],
        scratch_shapes=[pltpu.VMEM((4, block, block), jnp.float32)],
        compiler_params=pltpu.CompilerParams(vmem_limit_bytes=8 * 1024 * 1024),
        name="finish",
    )(
        *terms,
        diag_one.reshape(2, block, block),
        diag_two.reshape(block, block),
        coupling,
        near.astype(jnp.int32),
    )
    return (
        inv_one.reshape(factor_one.shape),
        out_one.reshape(diag_one.shape),
        inv_two.reshape(factor_two.shape),
        out_parent.reshape(parent_block.shape),
        out_two.reshape(diag_two.shape),
    )


def solution(mesh):
    placed = (
        P(None, "row", None, None, "col", None),
        P(None, "row", None, None, "col", None),
        P(None, "row", None, None, "col", None),
        P(None, "col", None, None),
        P(None, "col", None, None),
        P(None, "col", None, None),
        P(None, "row", None, "col"),
        P(None, "row", None, "col"),
        P(None, "col"),
    )
    return jax.shard_map(
        body,
        mesh=mesh,
        in_specs=placed,
        out_specs=(
            P(None, "row", None, None, "col", None),
            P(None, "col", None, None),
            P(None, "row", None, None, "col", None),
            P(None, "col", None, None),
            P(None, "col", None, None),
        ),
        check_vma=False,
    )
```

```python
import functools

import jax
import jax.numpy as jnp
from jax import lax
from jax.experimental import pallas as pl
from jax.experimental.pallas import tpu as pltpu
from jax.sharding import PartitionSpec as P

AXES = ("row", "col")


def send(value, sizes, source):
    high, wide = sizes
    pairs = []
    for z in range(high):
        for y in range(2):
            for x in range(wide):
                for k in range(2):
                    sz, sy, sx, sk = source(z, y, x, k)
                    pairs.append(
                        ((2 * sz + sy) * 2 * wide + 2 * sx + sk, (2 * z + y) * 2 * wide + 2 * x + k)
                    )
    return lax.ppermute(value, AXES, pairs)


def place():
    row, col = lax.axis_index("row"), lax.axis_index("col")
    return row // 2, row % 2, col // 2, col % 2


def tdot(left, right):
    return lax.dot_general(
        left, right, (((0,), (0,)), ((), ())), preferred_element_type=jnp.float32
    )


def product_kernel(high, wide, *refs):
    near_refs, far_refs = refs[:2], refs[2 : wide + 1]
    refs = refs[wide + 1 :]
    x_refs, other_ref, refs = refs[: 3 * high // 2 - 1], refs[3 * high // 2 - 1], refs[3 * high // 2 :]
    keep_y, send_y, keep_g, send_g, a_all, x_all, x_row, y_all, g_all = refs
    block = other_ref.shape[0]
    z, y, x, k = place()
    low = z % 2
    turn = z ^ x
    swap = y ^ k
    width = 3 * block
    couple = x_refs[0][:, width:]
    source = iter(x_refs)
    for step in range(high):
        rows = pl.ds(pl.multiple_of((turn ^ step) * block, block), block)
        if step < 3 or step % 2 == 0:
            x_all[rows, :] = next(source)[:, :width]
        else:
            x_all[rows, : 2 * block] = next(source)[...]
            x_all[rows, 2 * block :] = next(source)[...]
    for dy in range(2):
        for dx in range(wide):
            for kk in range(2):
                t = kk * wide + dx
                a_all[dy * block : (dy + 1) * block, t * block : (t + 1) * block] = (
                    far_refs[dx - 1][dy, kk] if dx else near_refs[dy][kk]
                )
    x_row[pl.ds(pl.multiple_of(swap * block, block), block), :] = x_refs[0][:, :width]
    x_row[pl.ds(pl.multiple_of((1 - swap) * block, block), block), :] = other_ref[:, :width]
    total = jnp.dot(a_all[...], x_all[...], preferred_element_type=jnp.float32)
    near = total[:, :block].astype(jnp.bfloat16)
    far = total[:, block : 2 * block]
    last = total[:, 2 * block :] - jnp.dot(
        near, couple, preferred_element_type=jnp.float32
    )
    y_all[:, : 2 * block] = total[:, : 2 * block]
    y_all[:, 2 * block :] = last
    g_all[0] = tdot(x_row[:, :block], near)
    g_all[1] = tdot(x_row[:, block : 2 * block], far.astype(jnp.bfloat16))
    g_all[2] = tdot(near, x_row[:, 2 * block :])
    g_all[3] = tdot(x_row[:, 2 * block :], last.astype(jnp.bfloat16))
    keep_y[...] = y_all[pl.ds(pl.multiple_of(swap * block, block), block), :]
    send_y[...] = y_all[pl.ds(pl.multiple_of((1 - swap) * block, block), block), :]
    keep_g[:block] = g_all[2 * k + low]
    keep_g[block:] = g_all[2 * k + 1 - low]
    send_g[:block] = g_all[2 * (1 - k) + low].astype(jnp.bfloat16)
    send_g[block:] = g_all[2 * (1 - k) + 1 - low].astype(jnp.bfloat16)


def inverse_kernel(y_ref, which_ref, one_ref, two_ref, out_one, out_two):
    block = y_ref.shape[0]
    flip = which_ref[0] == 1
    near, far = y_ref[:, :block], y_ref[:, block : 2 * block]
    zero = jnp.where(flip, far, near)
    unit = jnp.where(flip, near, far)
    out_one[:, 0, :] = jnp.where(one_ref[0] != 0, -zero, jnp.zeros_like(zero))
    out_one[:, 1, :] = jnp.where(one_ref[1] != 0, -unit, jnp.zeros_like(unit))
    last = y_ref[:, 2 * block :]
    out_two[...] = jnp.where(two_ref[0] != 0, -last, jnp.zeros_like(last))


def finish_kernel(*refs):
    got_refs = refs[:4]
    one_ref, two_ref, couple_ref, which_ref, out_one, out_parent, out_two, terms = refs[4:]
    z, y, x, k = place()
    low = z % 2
    for i, ref in enumerate(got_refs):
        terms[2 * (y ^ (i % 2)) + (low ^ (i // 2))] = ref[...].astype(jnp.float32)
    near = which_ref[0]
    one = one_ref[near] + terms[0]
    out_one[near] = one
    out_one[1 - near] = one_ref[1 - near] + terms[1]
    couple = couple_ref[...]
    parent = -(
        jnp.dot(one.astype(jnp.bfloat16), couple, preferred_element_type=jnp.float32) - terms[2]
    )
    parent = parent.astype(jnp.bfloat16)
    out_parent[...] = parent
    out_two[...] = two_ref[...] + terms[3] - tdot(couple, parent)


def body(
    anc_inverse,
    factor_one,
    factor_two,
    parent_block,
    diag_one,
    diag_two,
    pattern_one,
    pattern_two,
    parent,
):
    block = anc_inverse.shape[2]
    high = lax.axis_size("row") // 2
    wide = lax.axis_size("col") // 2
    sizes = (high, wide)
    z, y, x, k = place()
    near = parent.reshape(1) // lax.axis_size("col")
    keep_one = pattern_one.reshape(2)
    keep_two = pattern_two.reshape(1)
    flip = near[0] == 1
    one = factor_one.reshape(block, 2, block)
    one = jnp.where(keep_one[None, :, None] != 0, one, jnp.bfloat16(0))
    zero, unit = one[:, 0], one[:, 1]
    pair = jnp.concatenate([jnp.where(flip, unit, zero), jnp.where(flip, zero, unit)], axis=1)
    last = factor_two.reshape(block, block) * keep_two[0].astype(jnp.bfloat16)
    cols = jnp.concatenate([pair, last], axis=1)
    coupling = parent_block.reshape(block, block)
    anc = anc_inverse.reshape(block, 2, block).transpose(1, 0, 2)

    def plane(value, dy, dx):
        return send(value, sizes, lambda z, y, x, k: (z, y ^ dy, x ^ dx, k))

    def across(value, d):
        return send(value, sizes, lambda z, y, x, k: (z ^ d, k, x, y))

    def along(value, d):
        return send(value, sizes, lambda z, y, x, k: (z ^ d, y, x, k))

    pieces = {d: across(cols, d) for d in [*range(2, high, 2), 1]}
    own = across(jnp.concatenate([cols, coupling], axis=1), 0)
    now = anc
    near_anc = [anc, plane(now, 1, 0)]
    stacked = jnp.stack(near_anc)
    far_anc = [plane(stacked, 0, dx) for dx in range(1, wide)]
    for d in range(3, high, 2):
        pieces[d] = (
            along(pieces[d - 1][:, : 2 * block], 1),
            along(pieces[1][:, 2 * block :], d - 1),
        )
    cols_now = cols
    other = send(cols_now, sizes, lambda z, y, x, k: (z, 1 - k, x, y))
    pieces = [own] + [p for d in range(1, high) for p in (pieces[d] if d in range(3, high, 2) else (pieces[d],))]
    width = 3 * block
    keep_y, send_y, keep_g, send_g = pl.pallas_call(
        functools.partial(product_kernel, high, wide),
        out_shape=(
            jax.ShapeDtypeStruct((block, width), jnp.float32),
            jax.ShapeDtypeStruct((block, width), jnp.float32),
            jax.ShapeDtypeStruct((2 * block, block), jnp.float32),
            jax.ShapeDtypeStruct((2 * block, block), jnp.bfloat16),
        ),
        scratch_shapes=[
            pltpu.VMEM((2 * block, high * block), jnp.bfloat16),
            pltpu.VMEM((high * block, width), jnp.bfloat16),
            pltpu.VMEM((2 * block, width), jnp.bfloat16),
            pltpu.VMEM((2 * block, width), jnp.float32),
            pltpu.VMEM((4, block, block), jnp.float32),
        ],
        compiler_params=pltpu.CompilerParams(vmem_limit_bytes=48 * 1024 * 1024),
        name="products",
    )(*near_anc, *far_anc, *pieces, other)

    def core_swap(value):
        return send(value, sizes, lambda z, y, x, k: (z, y, x, 1 - k))

    chip = keep_g + core_swap(send_g).astype(jnp.float32)
    total = chip[:block] + along(chip[block:].astype(jnp.bfloat16), 1).astype(jnp.float32)
    total = total.astype(jnp.bfloat16)
    d = 2
    while d < high:
        total = (total.astype(jnp.float32) + along(total, d).astype(jnp.float32)).astype(jnp.bfloat16)
        d *= 2
    terms = [
        send(total, sizes, lambda z, y, x, k, d=d, e=e: (z ^ d, k, x, y ^ e))
        for d in range(2)
        for e in range(2)
    ]

    row_y = (keep_y + core_swap(send_y)).astype(jnp.bfloat16)
    row_y = send(row_y, sizes, lambda z, y, x, k: (z, k, x, y))
    inv_one, inv_two = pl.pallas_call(
        inverse_kernel,
        out_shape=(
            jax.ShapeDtypeStruct((block, 2, block), jnp.bfloat16),
            jax.ShapeDtypeStruct((block, block), jnp.bfloat16),
        ),
        in_specs=[pl.BlockSpec(memory_space=pltpu.VMEM)] + [pl.BlockSpec(memory_space=pltpu.SMEM)] * 3,
        compiler_params=pltpu.CompilerParams(vmem_limit_bytes=8 * 1024 * 1024),
        name="inverse",
    )(row_y, near.astype(jnp.int32), keep_one, keep_two)
    terms[0], inv_one, inv_two = lax.optimization_barrier((terms[0], inv_one, inv_two))

    out_one, out_parent, out_two = pl.pallas_call(
        finish_kernel,
        out_shape=(
            jax.ShapeDtypeStruct((2, block, block), jnp.float32),
            jax.ShapeDtypeStruct((block, block), jnp.bfloat16),
            jax.ShapeDtypeStruct((block, block), jnp.float32),
        ),
        in_specs=[pl.BlockSpec(memory_space=pltpu.VMEM)] * 7
        + [pl.BlockSpec(memory_space=pltpu.SMEM)],
        scratch_shapes=[pltpu.VMEM((4, block, block), jnp.float32)],
        compiler_params=pltpu.CompilerParams(vmem_limit_bytes=8 * 1024 * 1024),
        name="finish",
    )(
        *terms,
        diag_one.reshape(2, block, block),
        diag_two.reshape(block, block),
        coupling,
        near.astype(jnp.int32),
    )
    return (
        inv_one.reshape(factor_one.shape),
        out_one.reshape(diag_one.shape),
        inv_two.reshape(factor_two.shape),
        out_parent.reshape(parent_block.shape),
        out_two.reshape(diag_two.shape),
    )


def solution(mesh):
    placed = (
        P(None, "row", None, None, "col", None),
        P(None, "row", None, None, "col", None),
        P(None, "row", None, None, "col", None),
        P(None, "col", None, None),
        P(None, "col", None, None),
        P(None, "col", None, None),
        P(None, "row", None, "col"),
        P(None, "row", None, "col"),
        P(None, "col"),
    )
    return jax.shard_map(
        body,
        mesh=mesh,
        in_specs=placed,
        out_specs=(
            P(None, "row", None, None, "col", None),
            P(None, "col", None, None),
            P(None, "row", None, None, "col", None),
            P(None, "col", None, None),
            P(None, "col", None, None),
        ),
        check_vma=False,
    )
```

```python
import functools

import jax
import jax.numpy as jnp
from jax import lax
from jax.experimental import pallas as pl
from jax.experimental.pallas import tpu as pltpu
from jax.sharding import PartitionSpec as P

AXES = ("row", "col")


def send(value, sizes, source):
    high, wide = sizes
    pairs = []
    for z in range(high):
        for y in range(2):
            for x in range(wide):
                for k in range(2):
                    sz, sy, sx, sk = source(z, y, x, k)
                    pairs.append(
                        ((2 * sz + sy) * 2 * wide + 2 * sx + sk, (2 * z + y) * 2 * wide + 2 * x + k)
                    )
    return lax.ppermute(value, AXES, pairs)


def place():
    row, col = lax.axis_index("row"), lax.axis_index("col")
    return row // 2, row % 2, col // 2, col % 2


def copy_kernel(source_ref, out_ref):
    out_ref[...] = source_ref[...]


def tdot(left, right):
    return lax.dot_general(
        left, right, (((0,), (0,)), ((), ())), preferred_element_type=jnp.float32
    )


def product_kernel(high, wide, *refs):
    near_refs, far_refs = refs[:2], refs[2 : wide + 1]
    refs = refs[wide + 1 :]
    x_refs, other_ref, refs = refs[: 3 * high // 2 - 1], refs[3 * high // 2 - 1], refs[3 * high // 2 :]
    keep_y, send_y, keep_g, send_g, a_all, x_all, x_row, y_all, g_all = refs
    block = other_ref.shape[0]
    z, y, x, k = place()
    low = z % 2
    turn = z ^ x
    swap = y ^ k
    width = 3 * block
    couple = x_refs[0][:, width:]
    source = iter(x_refs)
    for step in range(high):
        rows = pl.ds(pl.multiple_of((turn ^ step) * block, block), block)
        if step < 3 or step % 2 == 0:
            x_all[rows, :] = next(source)[:, :width]
        else:
            x_all[rows, : 2 * block] = next(source)[...]
            x_all[rows, 2 * block :] = next(source)[...]
    for dy in range(2):
        for dx in range(wide):
            for kk in range(2):
                t = kk * wide + dx
                a_all[dy * block : (dy + 1) * block, t * block : (t + 1) * block] = (
                    far_refs[dx - 1][dy, kk] if dx else near_refs[dy][kk]
                )
    x_row[pl.ds(pl.multiple_of(swap * block, block), block), :] = x_refs[0][:, :width]
    x_row[pl.ds(pl.multiple_of((1 - swap) * block, block), block), :] = other_ref[:, :width]
    total = jnp.dot(a_all[...], x_all[...], preferred_element_type=jnp.float32)
    near = total[:, :block].astype(jnp.bfloat16)
    far = total[:, block : 2 * block]
    last = total[:, 2 * block :] - jnp.dot(
        near, couple, preferred_element_type=jnp.float32
    )
    y_all[:, : 2 * block] = total[:, : 2 * block]
    y_all[:, 2 * block :] = last
    g_all[0] = tdot(x_row[:, :block], near)
    g_all[1] = tdot(x_row[:, block : 2 * block], far.astype(jnp.bfloat16))
    g_all[2] = tdot(near, x_row[:, 2 * block :])
    g_all[3] = tdot(x_row[:, 2 * block :], last.astype(jnp.bfloat16))
    keep_y[...] = y_all[pl.ds(pl.multiple_of(swap * block, block), block), :]
    send_y[...] = y_all[pl.ds(pl.multiple_of((1 - swap) * block, block), block), :]
    keep_g[:block] = g_all[2 * k + low]
    keep_g[block:] = g_all[2 * k + 1 - low]
    send_g[:block] = g_all[2 * (1 - k) + low].astype(jnp.bfloat16)
    send_g[block:] = g_all[2 * (1 - k) + 1 - low].astype(jnp.bfloat16)


def inverse_kernel(y_ref, which_ref, one_ref, two_ref, out_one, out_two):
    block = y_ref.shape[0]
    flip = which_ref[0] == 1
    near, far = y_ref[:, :block], y_ref[:, block : 2 * block]
    zero = jnp.where(flip, far, near)
    unit = jnp.where(flip, near, far)
    out_one[:, 0, :] = jnp.where(one_ref[0] != 0, -zero, jnp.zeros_like(zero))
    out_one[:, 1, :] = jnp.where(one_ref[1] != 0, -unit, jnp.zeros_like(unit))
    last = y_ref[:, 2 * block :]
    out_two[...] = jnp.where(two_ref[0] != 0, -last, jnp.zeros_like(last))


def finish_kernel(*refs):
    got_refs = refs[:4]
    one_ref, two_ref, couple_ref, which_ref, out_one, out_parent, out_two, terms = refs[4:]
    z, y, x, k = place()
    low = z % 2
    for i, ref in enumerate(got_refs):
        terms[2 * (y ^ (i % 2)) + (low ^ (i // 2))] = ref[...].astype(jnp.float32)
    near = which_ref[0]
    one = one_ref[near] + terms[0]
    out_one[near] = one
    out_one[1 - near] = one_ref[1 - near] + terms[1]
    couple = couple_ref[...]
    parent = -(
        jnp.dot(one.astype(jnp.bfloat16), couple, preferred_element_type=jnp.float32) - terms[2]
    )
    parent = parent.astype(jnp.bfloat16)
    out_parent[...] = parent
    out_two[...] = two_ref[...] + terms[3] - tdot(couple, parent)


def body(
    anc_inverse,
    factor_one,
    factor_two,
    parent_block,
    diag_one,
    diag_two,
    pattern_one,
    pattern_two,
    parent,
):
    block = anc_inverse.shape[2]
    high = lax.axis_size("row") // 2
    wide = lax.axis_size("col") // 2
    sizes = (high, wide)
    z, y, x, k = place()
    near = parent.reshape(1) // lax.axis_size("col")
    keep_one = pattern_one.reshape(2)
    keep_two = pattern_two.reshape(1)
    flip = near[0] == 1
    one = factor_one.reshape(block, 2, block)
    one = jnp.where(keep_one[None, :, None] != 0, one, jnp.bfloat16(0))
    zero, unit = one[:, 0], one[:, 1]
    pair = jnp.concatenate([jnp.where(flip, unit, zero), jnp.where(flip, zero, unit)], axis=1)
    last = factor_two.reshape(block, block) * keep_two[0].astype(jnp.bfloat16)
    cols = jnp.concatenate([pair, last], axis=1)
    coupling = parent_block.reshape(block, block)
    anc = anc_inverse.reshape(block, 2, block).transpose(1, 0, 2)

    def plane(value, dy, dx):
        return send(value, sizes, lambda z, y, x, k: (z, y ^ dy, x ^ dx, k))

    def across(value, d):
        return send(value, sizes, lambda z, y, x, k: (z ^ d, k, x, y))

    def along(value, d):
        return send(value, sizes, lambda z, y, x, k: (z ^ d, y, x, k))

    def staged(value, flops):
        return pl.pallas_call(
            copy_kernel,
            out_shape=jax.ShapeDtypeStruct(value.shape, value.dtype),
            cost_estimate=pl.CostEstimate(
                flops=flops, bytes_accessed=4 * value.size, transcendentals=0
            ),
            compiler_params=pltpu.CompilerParams(vmem_limit_bytes=4 * 1024 * 1024),
            name="stage",
        )(value)

    pieces = {d: across(cols, d) for d in [*range(2, high, 2), 1]}
    own = across(jnp.concatenate([cols, coupling], axis=1), 0)
    now = anc
    near_anc = [anc, plane(now, 1, 0)]
    stacked = jnp.stack(near_anc)
    far_anc = [plane(stacked, 0, dx) for dx in range(1, wide)]
    for d in range(3, high, 2):
        pieces[d] = (
            staged(along(pieces[d - 1][:, : 2 * block], 1), 2*10**9),
            along(pieces[1][:, 2 * block :], d - 1),
        )
    cols_now = cols
    other = send(cols_now, sizes, lambda z, y, x, k: (z, 1 - k, x, y))
    pieces = [own] + [p for d in range(1, high) for p in (pieces[d] if d in range(3, high, 2) else (pieces[d],))]
    width = 3 * block
    keep_y, send_y, keep_g, send_g = pl.pallas_call(
        functools.partial(product_kernel, high, wide),
        out_shape=(
            jax.ShapeDtypeStruct((block, width), jnp.float32),
            jax.ShapeDtypeStruct((block, width), jnp.float32),
            jax.ShapeDtypeStruct((2 * block, block), jnp.float32),
            jax.ShapeDtypeStruct((2 * block, block), jnp.bfloat16),
        ),
        scratch_shapes=[
            pltpu.VMEM((2 * block, high * block), jnp.bfloat16),
            pltpu.VMEM((high * block, width), jnp.bfloat16),
            pltpu.VMEM((2 * block, width), jnp.bfloat16),
            pltpu.VMEM((2 * block, width), jnp.float32),
            pltpu.VMEM((4, block, block), jnp.float32),
        ],
        compiler_params=pltpu.CompilerParams(vmem_limit_bytes=48 * 1024 * 1024),
        name="products",
    )(*near_anc, *far_anc, *pieces, other)

    def core_swap(value):
        return send(value, sizes, lambda z, y, x, k: (z, y, x, 1 - k))

    chip = keep_g + core_swap(send_g).astype(jnp.float32)
    total = chip[:block] + along(chip[block:].astype(jnp.bfloat16), 1).astype(jnp.float32)
    total = total.astype(jnp.bfloat16)
    d = 2
    while d < high:
        total = (total.astype(jnp.float32) + along(total, d).astype(jnp.float32)).astype(jnp.bfloat16)
        d *= 2
    terms = [
        send(total, sizes, lambda z, y, x, k, d=d, e=e: (z ^ d, k, x, y ^ e))
        for d in range(2)
        for e in range(2)
    ]

    row_y = (keep_y + core_swap(send_y)).astype(jnp.bfloat16)
    row_y = send(row_y, sizes, lambda z, y, x, k: (z, k, x, y))
    inv_one, inv_two = pl.pallas_call(
        inverse_kernel,
        out_shape=(
            jax.ShapeDtypeStruct((block, 2, block), jnp.bfloat16),
            jax.ShapeDtypeStruct((block, block), jnp.bfloat16),
        ),
        in_specs=[pl.BlockSpec(memory_space=pltpu.VMEM)] + [pl.BlockSpec(memory_space=pltpu.SMEM)] * 3,
        compiler_params=pltpu.CompilerParams(vmem_limit_bytes=8 * 1024 * 1024),
        name="inverse",
    )(row_y, near.astype(jnp.int32), keep_one, keep_two)
    terms[0], inv_one, inv_two = lax.optimization_barrier((terms[0], inv_one, inv_two))

    out_one, out_parent, out_two = pl.pallas_call(
        finish_kernel,
        out_shape=(
            jax.ShapeDtypeStruct((2, block, block), jnp.float32),
            jax.ShapeDtypeStruct((block, block), jnp.bfloat16),
            jax.ShapeDtypeStruct((block, block), jnp.float32),
        ),
        in_specs=[pl.BlockSpec(memory_space=pltpu.VMEM)] * 7
        + [pl.BlockSpec(memory_space=pltpu.SMEM)],
        scratch_shapes=[pltpu.VMEM((4, block, block), jnp.float32)],
        compiler_params=pltpu.CompilerParams(vmem_limit_bytes=8 * 1024 * 1024),
        name="finish",
    )(
        *terms,
        diag_one.reshape(2, block, block),
        diag_two.reshape(block, block),
        coupling,
        near.astype(jnp.int32),
    )
    return (
        inv_one.reshape(factor_one.shape),
        out_one.reshape(diag_one.shape),
        inv_two.reshape(factor_two.shape),
        out_parent.reshape(parent_block.shape),
        out_two.reshape(diag_two.shape),
    )


def solution(mesh):
    placed = (
        P(None, "row", None, None, "col", None),
        P(None, "row", None, None, "col", None),
        P(None, "row", None, None, "col", None),
        P(None, "col", None, None),
        P(None, "col", None, None),
        P(None, "col", None, None),
        P(None, "row", None, "col"),
        P(None, "row", None, "col"),
        P(None, "col"),
    )
    return jax.shard_map(
        body,
        mesh=mesh,
        in_specs=placed,
        out_specs=(
            P(None, "row", None, None, "col", None),
            P(None, "col", None, None),
            P(None, "row", None, None, "col", None),
            P(None, "col", None, None),
            P(None, "col", None, None),
        ),
        check_vma=False,
    )
```

```python
import functools

import jax
import jax.numpy as jnp
from jax import lax
from jax.experimental import pallas as pl
from jax.experimental.pallas import tpu as pltpu
from jax.sharding import PartitionSpec as P

AXES = ("row", "col")


def send(value, sizes, source):
    high, wide = sizes
    pairs = []
    for z in range(high):
        for y in range(2):
            for x in range(wide):
                for k in range(2):
                    sz, sy, sx, sk = source(z, y, x, k)
                    pairs.append(
                        ((2 * sz + sy) * 2 * wide + 2 * sx + sk, (2 * z + y) * 2 * wide + 2 * x + k)
                    )
    return lax.ppermute(value, AXES, pairs)


def place():
    row, col = lax.axis_index("row"), lax.axis_index("col")
    return row // 2, row % 2, col // 2, col % 2


def copy_kernel(source_ref, out_ref):
    out_ref[...] = source_ref[...]


def tdot(left, right):
    return lax.dot_general(
        left, right, (((0,), (0,)), ((), ())), preferred_element_type=jnp.float32
    )


def product_kernel(high, wide, *refs):
    near_refs, far_refs = refs[:2], refs[2 : wide + 1]
    refs = refs[wide + 1 :]
    x_refs, other_ref, refs = refs[: 3 * high // 2 - 1], refs[3 * high // 2 - 1], refs[3 * high // 2 :]
    keep_y, send_y, keep_g, send_g, a_all, x_all, x_row, y_all, g_all = refs
    block = other_ref.shape[0]
    z, y, x, k = place()
    low = z % 2
    turn = z ^ x
    swap = y ^ k
    width = 3 * block
    couple = x_refs[0][:, width:]
    source = iter(x_refs)
    for step in range(high):
        rows = pl.ds(pl.multiple_of((turn ^ step) * block, block), block)
        if step < 3 or step % 2 == 0:
            x_all[rows, :] = next(source)[:, :width]
        else:
            x_all[rows, : 2 * block] = next(source)[...]
            x_all[rows, 2 * block :] = next(source)[...]
    for dy in range(2):
        for dx in range(wide):
            for kk in range(2):
                t = kk * wide + dx
                a_all[dy * block : (dy + 1) * block, t * block : (t + 1) * block] = (
                    far_refs[dx - 1][dy, kk] if dx else near_refs[dy][kk]
                )
    x_row[pl.ds(pl.multiple_of(swap * block, block), block), :] = x_refs[0][:, :width]
    x_row[pl.ds(pl.multiple_of((1 - swap) * block, block), block), :] = other_ref[:, :width]
    total = jnp.dot(a_all[...], x_all[...], preferred_element_type=jnp.float32)
    near = total[:, :block].astype(jnp.bfloat16)
    far = total[:, block : 2 * block]
    last = total[:, 2 * block :] - jnp.dot(
        near, couple, preferred_element_type=jnp.float32
    )
    y_all[:, : 2 * block] = total[:, : 2 * block]
    y_all[:, 2 * block :] = last
    g_all[0] = tdot(x_row[:, :block], near)
    g_all[1] = tdot(x_row[:, block : 2 * block], far.astype(jnp.bfloat16))
    g_all[2] = tdot(near, x_row[:, 2 * block :])
    g_all[3] = tdot(x_row[:, 2 * block :], last.astype(jnp.bfloat16))
    keep_y[...] = y_all[pl.ds(pl.multiple_of(swap * block, block), block), :]
    send_y[...] = y_all[pl.ds(pl.multiple_of((1 - swap) * block, block), block), :]
    keep_g[:block] = g_all[2 * k + low]
    keep_g[block:] = g_all[2 * k + 1 - low]
    send_g[:block] = g_all[2 * (1 - k) + low].astype(jnp.bfloat16)
    send_g[block:] = g_all[2 * (1 - k) + 1 - low].astype(jnp.bfloat16)


def inverse_kernel(y_ref, which_ref, one_ref, two_ref, out_one, out_two):
    block = y_ref.shape[0]
    flip = which_ref[0] == 1
    near, far = y_ref[:, :block], y_ref[:, block : 2 * block]
    zero = jnp.where(flip, far, near)
    unit = jnp.where(flip, near, far)
    zero = jnp.where(one_ref[0] != 0, -zero, jnp.zeros_like(zero))
    unit = jnp.where(one_ref[1] != 0, -unit, jnp.zeros_like(unit))
    out_one[...] = jnp.stack([zero, unit], axis=1)
    last = y_ref[:, 2 * block :]
    out_two[...] = jnp.where(two_ref[0] != 0, -last, jnp.zeros_like(last))


def finish_kernel(*refs):
    got_refs = refs[:4]
    one_ref, two_ref, couple_ref, which_ref, out_one, out_parent, out_two, terms = refs[4:]
    z, y, x, k = place()
    low = z % 2
    for i, ref in enumerate(got_refs):
        terms[2 * (y ^ (i % 2)) + (low ^ (i // 2))] = ref[...].astype(jnp.float32)
    near = which_ref[0]
    one = one_ref[near] + terms[0]
    out_one[near] = one
    out_one[1 - near] = one_ref[1 - near] + terms[1]
    couple = couple_ref[...]
    parent = -(
        jnp.dot(one.astype(jnp.bfloat16), couple, preferred_element_type=jnp.float32) - terms[2]
    )
    parent = parent.astype(jnp.bfloat16)
    out_parent[...] = parent
    out_two[...] = two_ref[...] + terms[3] - tdot(couple, parent)


def body(
    anc_inverse,
    factor_one,
    factor_two,
    parent_block,
    diag_one,
    diag_two,
    pattern_one,
    pattern_two,
    parent,
):
    block = anc_inverse.shape[2]
    high = lax.axis_size("row") // 2
    wide = lax.axis_size("col") // 2
    sizes = (high, wide)
    z, y, x, k = place()
    near = parent.reshape(1) // lax.axis_size("col")
    keep_one = pattern_one.reshape(2)
    keep_two = pattern_two.reshape(1)
    flip = near[0] == 1
    one = factor_one.reshape(block, 2, block)
    one = jnp.where(keep_one[None, :, None] != 0, one, jnp.bfloat16(0))
    zero, unit = one[:, 0], one[:, 1]
    pair = jnp.concatenate([jnp.where(flip, unit, zero), jnp.where(flip, zero, unit)], axis=1)
    last = factor_two.reshape(block, block) * keep_two[0].astype(jnp.bfloat16)
    cols = jnp.concatenate([pair, last], axis=1)
    coupling = parent_block.reshape(block, block)
    anc = anc_inverse.reshape(block, 2, block).transpose(1, 0, 2)

    def plane(value, dy, dx):
        return send(value, sizes, lambda z, y, x, k: (z, y ^ dy, x ^ dx, k))

    def across(value, d):
        return send(value, sizes, lambda z, y, x, k: (z ^ d, k, x, y))

    def along(value, d):
        return send(value, sizes, lambda z, y, x, k: (z ^ d, y, x, k))

    def staged(value, flops):
        return pl.pallas_call(
            copy_kernel,
            out_shape=jax.ShapeDtypeStruct(value.shape, value.dtype),
            cost_estimate=pl.CostEstimate(
                flops=flops, bytes_accessed=4 * value.size, transcendentals=0
            ),
            compiler_params=pltpu.CompilerParams(vmem_limit_bytes=4 * 1024 * 1024),
            name="stage",
        )(value)

    pieces = {d: across(cols, d) for d in [*range(2, high, 2), 1]}
    own = across(jnp.concatenate([cols, coupling], axis=1), 0)
    now = anc
    near_anc = [anc, plane(now, 1, 0)]
    stacked = jnp.stack(near_anc)
    far_anc = [plane(stacked, 0, dx) for dx in range(1, wide)]
    for d in range(3, high, 2):
        pieces[d] = (
            staged(along(pieces[d - 1][:, : 2 * block], 1), 2*10**9),
            along(pieces[1][:, 2 * block :], d - 1),
        )
    cols_now = cols
    other = send(cols_now, sizes, lambda z, y, x, k: (z, 1 - k, x, y))
    pieces = [own] + [p for d in range(1, high) for p in (pieces[d] if d in range(3, high, 2) else (pieces[d],))]
    width = 3 * block
    keep_y, send_y, keep_g, send_g = pl.pallas_call(
        functools.partial(product_kernel, high, wide),
        out_shape=(
            jax.ShapeDtypeStruct((block, width), jnp.float32),
            jax.ShapeDtypeStruct((block, width), jnp.float32),
            jax.ShapeDtypeStruct((2 * block, block), jnp.float32),
            jax.ShapeDtypeStruct((2 * block, block), jnp.bfloat16),
        ),
        scratch_shapes=[
            pltpu.VMEM((2 * block, high * block), jnp.bfloat16),
            pltpu.VMEM((high * block, width), jnp.bfloat16),
            pltpu.VMEM((2 * block, width), jnp.bfloat16),
            pltpu.VMEM((2 * block, width), jnp.float32),
            pltpu.VMEM((4, block, block), jnp.float32),
        ],
        compiler_params=pltpu.CompilerParams(vmem_limit_bytes=48 * 1024 * 1024),
        name="products",
    )(*near_anc, *far_anc, *pieces, other)

    def core_swap(value):
        return send(value, sizes, lambda z, y, x, k: (z, y, x, 1 - k))

    chip = keep_g + core_swap(send_g).astype(jnp.float32)
    total = chip[:block] + along(chip[block:].astype(jnp.bfloat16), 1).astype(jnp.float32)
    total = total.astype(jnp.bfloat16)
    d = 2
    while d < high:
        total = (total.astype(jnp.float32) + along(total, d).astype(jnp.float32)).astype(jnp.bfloat16)
        d *= 2
    terms = [
        send(total, sizes, lambda z, y, x, k, d=d, e=e: (z ^ d, k, x, y ^ e))
        for d in range(2)
        for e in range(2)
    ]

    row_y = (keep_y + core_swap(send_y)).astype(jnp.bfloat16)
    row_y = send(row_y, sizes, lambda z, y, x, k: (z, k, x, y))
    inv_one, inv_two = pl.pallas_call(
        inverse_kernel,
        out_shape=(
            jax.ShapeDtypeStruct((block, 2, block), jnp.bfloat16),
            jax.ShapeDtypeStruct((block, block), jnp.bfloat16),
        ),
        in_specs=[pl.BlockSpec(memory_space=pltpu.VMEM)] + [pl.BlockSpec(memory_space=pltpu.SMEM)] * 3,
        compiler_params=pltpu.CompilerParams(vmem_limit_bytes=8 * 1024 * 1024),
        name="inverse",
    )(row_y, near.astype(jnp.int32), keep_one, keep_two)
    terms[0], inv_one, inv_two = lax.optimization_barrier((terms[0], inv_one, inv_two))

    out_one, out_parent, out_two = pl.pallas_call(
        finish_kernel,
        out_shape=(
            jax.ShapeDtypeStruct((2, block, block), jnp.float32),
            jax.ShapeDtypeStruct((block, block), jnp.bfloat16),
            jax.ShapeDtypeStruct((block, block), jnp.float32),
        ),
        in_specs=[pl.BlockSpec(memory_space=pltpu.VMEM)] * 7
        + [pl.BlockSpec(memory_space=pltpu.SMEM)],
        scratch_shapes=[pltpu.VMEM((4, block, block), jnp.float32)],
        compiler_params=pltpu.CompilerParams(vmem_limit_bytes=8 * 1024 * 1024),
        name="finish",
    )(
        *terms,
        diag_one.reshape(2, block, block),
        diag_two.reshape(block, block),
        coupling,
        near.astype(jnp.int32),
    )
    return (
        inv_one.reshape(factor_one.shape),
        out_one.reshape(diag_one.shape),
        inv_two.reshape(factor_two.shape),
        out_parent.reshape(parent_block.shape),
        out_two.reshape(diag_two.shape),
    )


def solution(mesh):
    placed = (
        P(None, "row", None, None, "col", None),
        P(None, "row", None, None, "col", None),
        P(None, "row", None, None, "col", None),
        P(None, "col", None, None),
        P(None, "col", None, None),
        P(None, "col", None, None),
        P(None, "row", None, "col"),
        P(None, "row", None, "col"),
        P(None, "col"),
    )
    return jax.shard_map(
        body,
        mesh=mesh,
        in_specs=placed,
        out_specs=(
            P(None, "row", None, None, "col", None),
            P(None, "col", None, None),
            P(None, "row", None, None, "col", None),
            P(None, "col", None, None),
            P(None, "col", None, None),
        ),
        check_vma=False,
    )
```
